512 devices in a mesh: tm: 32 (over z_lo, y), feat: 16 (over x, z_hi, core).
Axes of the slice: x: 4, y: 4, z: 16 (z_hi: 2, z_lo: 8; z = z_hi * 8 + z_lo), core: 2. Of those that a mesh axis runs over, the one named last changes fastest.
Arguments:
- frames: bfloat16 [24576, 8192], P('tm', 'feat'), may hold values from -6 to 6
Outputs:
- instant: float32 [8192, 2, 512], P(('feat', 'tm'))
- lagged_cov: float32 [8192, 2, 512], P(('feat', 'tm'))
The draws below stay inside these ranges and needn't reach their ends.
All inputs are finite; a program needn't handle non-finite values.
Results may differ from the reference program's by a relative error of at most 0.0003.
Values may be sent and summed in bfloat16 or wider, within the bound.
A program may use at most 64 MiB of HBM per device.

```python
import math
import jax
import jax.numpy as jnp
from jax import lax

F = 8192
LAG = 256
STEPS = 2
FRAMES = 24576
P_SIZE = 512
N_FEAT = 16


def raised(result, own_key, source, target, shards_of, factor):
    owner, partner = [(jnp.arange(result.shape[dim]) // (result.shape[dim] // shards_of)).reshape([-1 if axis == dim else 1 for axis in range(result.ndim)]) for dim in (source, target)]
    chosen = jax.random.permutation(own_key, shards_of)[partner]
    strong = (owner == chosen) | (owner == (partner + shards_of // 2) % shards_of)
    return jnp.where(strong, factor * result, result)


def block_levels(rng, shape, pieces, smallest, top_value):
    gain = 1.0
    for axis_at, blocks in pieces:
        draws = jax.random.uniform(jax.random.fold_in(jax.random.fold_in(rng, 6), axis_at), (blocks,), jnp.float32, smallest / len(pieces), top_value / len(pieces))
        gain = gain * jnp.repeat(jnp.exp(draws), shape[axis_at] // blocks).reshape((-1,) + (1,) * (len(shape) - 1 - axis_at))
    return gain


def gaussian_with(key, dims, width, limit, split, heavy, held_as=jnp.bfloat16):
    values = width * jax.random.normal(key, dims, jnp.float32)
    if split:
        values = values * block_levels(key, dims, split, -0.22, 0.18)
    return jnp.clip(raised(values, jax.random.fold_in(key, 3), *heavy), -limit, limit).astype(held_as)


def setup_inputs(seed: int = 0) -> dict:
    splits = jax.random.split(jax.random.key(seed), 2)
    frames = gaussian_with(splits[0], (FRAMES, F), 1.0, 6.0, ((0, 32), (1, 16)), (0, 1, 32, 2.75))
    return dict(frames=frames)


def reference(frames):
    data = frames.astype(jnp.float32)
    later = jnp.concatenate([data[LAG:], jnp.zeros((LAG, F), jnp.float32)], axis=0)
    norm_scale = 1.0 / math.sqrt(FRAMES)
    zero_rows = []
    lag_rows = []
    for panel in range(N_FEAT):
        columns = data[:, panel * P_SIZE:(panel + 1) * P_SIZE]
        zero_parts = []
        lag_parts = []
        for step in range(STEPS):
            other = (panel + step) % N_FEAT * P_SIZE
            zero_parts.append(jnp.dot(columns.T, data[:, other:other + P_SIZE], precision=lax.Precision.HIGHEST))
            lag_parts.append(jnp.dot(columns.T, later[:, other:other + P_SIZE], precision=lax.Precision.HIGHEST))
        zero_rows.append(jnp.stack(zero_parts, axis=1))
        lag_rows.append(jnp.stack(lag_parts, axis=1))
    instant = jnp.concatenate(zero_rows, axis=0) * norm_scale
    lagged_cov = jnp.concatenate(lag_rows, axis=0) * norm_scale
    return (instant, lagged_cov)
```

```python
import functools
import math

import jax
import jax.numpy as jnp
from jax import lax
from jax.experimental import pallas as pl
from jax.experimental.pallas import tpu as pltpu
from jax.sharding import PartitionSpec as P

LAG = 256
ROWS = 768
WIDTH = 512
NC = 2
C = WIDTH // NC
UNITS = 2 * NC
NY = 4
PEAK = 2.0**8.4
MESH = pl.DeviceIdType.MESH


def encode(part, dst):
    n = part.shape[0]
    grouped = part.reshape(n // 32, 2, 16, part.shape[1])
    top = jnp.max(jnp.max(jnp.abs(grouped), axis=0), axis=1, keepdims=True)
    scale = jnp.maximum(top, 1e-36).astype(jnp.bfloat16)
    unit = grouped * (PEAK / scale.astype(jnp.float32))[None]
    third = unit * unit * unit
    sixth = third * third
    code = (sixth * sixth * third).reshape(n, part.shape[1])
    dst[pl.ds(0, n), :] = code.astype(jnp.bfloat16)
    wide = jnp.broadcast_to(scale.astype(jnp.float32), (2, 8, part.shape[1]))
    dst[pl.ds(n, 16), :] = wide.reshape(16, part.shape[1]).astype(jnp.bfloat16)


def decode(src):
    n, width = src.shape[0] - 16, src.shape[1]
    code = src[pl.ds(0, n), :].astype(jnp.float32)
    scale = src[pl.ds(n, 16), :].astype(jnp.float32).reshape(2, 8, width)[:, :1]
    size = jnp.exp2(jnp.log2(jnp.abs(code)) * (1.0 / 15.0))
    value = jnp.where(code > 0, size, jnp.where(code < 0, -size, 0.0))
    value = value.reshape(n // 32, 2, 16, width) * (scale * (1.0 / PEAK))[None]
    return value.reshape(n, width)


def kernel(
    norm_scale, count_tm, count_feat,
    a_hbm, inst_ref, lag_ref,
    panels, left, tail, acc, ysend, yrecv, z1send, z1recv, z2send, z2recv, z3send, z3recv, half1, half2, half3,
    load_sem, psend, precv, tsem, ysem_s, ysem_r, zsem_s, zsem_r,
):
    tm, feat = lax.axis_index("tm"), lax.axis_index("feat")
    zl, y = tm // NY, tm % NY
    b0, b1, b2 = zl % 2, (zl // 2) % 2, zl // 4
    before = (tm, (feat + count_feat - 1) % count_feat)
    after = (tm, (feat + 1) % count_feat)
    ypeer = [((zl * NY) + (y + j) % NY, feat) for j in range(NY)]
    zpeer = [
        ((zl + step * (1 - 2 * bit)) * NY + y, feat) for step, bit in ((1, b0), (2, b1), (4, b2))
    ]

    loads = [
        pltpu.make_async_copy(a_hbm.at[:, pl.ds(c * C, C)], panels.at[c], load_sem.at[c]) for c in range(NC)
    ]
    for load in loads:
        load.start()

    barrier = pltpu.get_barrier_semaphore()
    for peer in ypeer[1:] + zpeer + [after]:
        pl.semaphore_signal(barrier, inc=1, device_id=peer, device_id_type=MESH)

    @pl.when(tm > 0)
    def _():
        pl.semaphore_signal(barrier, inc=1, device_id=(tm - 1, feat), device_id_type=MESH)

    pl.semaphore_wait(barrier, 8 - (tm + 1) // count_tm)

    def pass_panel(c):
        return pltpu.make_async_remote_copy(
            src_ref=panels.at[c], dst_ref=panels.at[NC + c], send_sem=psend.at[c], recv_sem=precv.at[c],
            device_id=before, device_id_type=MESH,
        )

    def pass_tail(target):
        return pltpu.make_async_remote_copy(
            src_ref=a_hbm.at[pl.ds(ROWS - LAG, LAG)], dst_ref=tail, send_sem=tsem.at[0], recv_sem=tsem.at[1],
            device_id=target, device_id_type=MESH,
        )

    for c in range(NC):
        loads[c].wait()
        pass_panel(c).start()

    @pl.when(tm < count_tm - 1)
    def _():
        pass_tail((tm + 1, feat)).start()

    def row_of(block, owner_y):
        bits = (block % 2) * 4 + (block // 2 % 2) * 2 + block // 4
        return owner_y * 256 + bits * 32

    per = C // 128
    for j in range(WIDTH // 128):
        cols = panels[j // per, :, pl.ds((j % per) * 128, 128)].T
        for p in range(2):
            for owner in range(NY):
                at = row_of(2 * j + p, owner)
                piece = cols[p * 64 + owner * 16 : p * 64 + owner * 16 + 16]
                left[pl.ds(at, 16), :] = piece
                left[pl.ds(at + 16, 16), pl.ds(LAG, ROWS - LAG)] = piece[:, : ROWS - LAG]

    @pl.when(tm == 0)
    def _():
        tail[...] = jnp.zeros_like(tail)

    @pl.when(tm > 0)
    def _():
        pass_tail((tm, feat)).wait_recv()

    for j in range(WIDTH // 128):
        cols = tail[:, pl.ds(j * 128, 128)].T
        for p in range(2):
            for owner in range(NY):
                at = row_of(2 * j + p, owner)
                left[pl.ds(at + 16, 16), pl.ds(0, LAG)] = cols[p * 64 + owner * 16 : p * 64 + owner * 16 + 16]

    def pass_y(u, j):
        return pltpu.make_async_remote_copy(
            src_ref=ysend.at[u, j - 1], dst_ref=yrecv.at[u, j - 1], send_sem=ysem_s.at[u, j - 1],
            recv_sem=ysem_r.at[u, j - 1], device_id=ypeer[j], device_id_type=MESH,
        )

    def product(u, j):
        owner = (y + j) % NY
        rows = left[pl.ds(pl.multiple_of(owner * 256, 256), 256), :]
        return jnp.dot(rows, panels[u], preferred_element_type=jnp.float32)

    def multiply(u):
        if u >= NC:
            pass_panel(u - NC).wait_recv()
        for j in range(1, NY):
            encode(product(u, j), ysend.at[u, j - 1])
            pass_y(u, j).start()
        acc[u] = product(u, 0)

    def sum_y(u):
        for j in range(1, NY):
            pass_y(u, j).wait_recv()
            acc[u] += decode(yrecv.at[u, j - 1])

    def pass_z(u, k, src, dst):
        return pltpu.make_async_remote_copy(
            src_ref=src.at[u], dst_ref=dst.at[u], send_sem=zsem_s.at[u, k], recv_sem=zsem_r.at[u, k],
            device_id=zpeer[k], device_id_type=MESH,
        )

    def part(ref, u, bit, n):
        return ref[u, pl.ds(pl.multiple_of(bit * n, n), n), :]

    def z1(u):
        encode(part(acc, u, 1 - b0, 128), z1send.at[u])
        pass_z(u, 0, z1send, z1recv).start()

    def z2(u):
        pass_z(u, 0, z1send, z1recv).wait_recv()
        half1[u] = part(acc, u, b0, 128) + decode(z1recv.at[u])
        encode(part(half1, u, 1 - b1, 64), z2send.at[u])
        pass_z(u, 1, z2send, z2recv).start()

    def z3(u):
        pass_z(u, 1, z2send, z2recv).wait_recv()
        half2[u] = part(half1, u, b1, 64) + decode(z2recv.at[u])
        z3send[u] = part(half2, u, 1 - b2, 32)
        pass_z(u, 2, z3send, z3recv).start()

    def finish(u):
        pass_z(u, 2, z3send, z3recv).wait_recv()
        done = (part(half2, u, b2, 32) + z3recv[u]) * norm_scale
        s, at = u // NC, (u % NC) * C
        inst_ref[:, s, pl.ds(at, C)] = done[:16]
        lag_ref[:, s, pl.ds(at, C)] = done[16:]

    for u in range(UNITS):
        multiply(u)
        if u < UNITS - 1 and u > 0:
            sum_y(u - 1)
    for c in range(NC):
        pass_panel(c).wait_send()
    for u in range(UNITS):
        if u >= UNITS - 2:
            sum_y(u)
        z1(u)
    for step in (z2, z3, finish):
        for u in range(UNITS):
            step(u)

    for u in range(UNITS):
        for j in range(1, NY):
            pass_y(u, j).wait_send()
        pass_z(u, 0, z1send, z1recv).wait_send()
        pass_z(u, 1, z2send, z2recv).wait_send()
        pass_z(u, 2, z3send, z3recv).wait_send()

    @pl.when(tm < count_tm - 1)
    def _():
        pass_tail((tm + 1, feat)).wait_send()


def shards(count_tm, count_feat, frames):
    norm_scale = 1.0 / math.sqrt(ROWS * count_tm)
    f32, bf16, sem = jnp.float32, jnp.bfloat16, pltpu.SemaphoreType.DMA
    out = jax.ShapeDtypeStruct((16, 2, WIDTH), f32)
    return pl.pallas_call(
        functools.partial(kernel, norm_scale, count_tm, count_feat),
        out_shape=(out, out),
        in_specs=[pl.BlockSpec(memory_space=pl.ANY)],
        out_specs=(pl.BlockSpec(memory_space=pltpu.VMEM), pl.BlockSpec(memory_space=pltpu.VMEM)),
        scratch_shapes=[
            pltpu.VMEM((UNITS, ROWS, C), bf16),
            pltpu.VMEM((NY * 256, ROWS), bf16),
            pltpu.VMEM((LAG, WIDTH), bf16),
            pltpu.VMEM((UNITS, 256, C), f32),
            pltpu.VMEM((UNITS, NY - 1, 256 + 16, C), bf16),
            pltpu.VMEM((UNITS, NY - 1, 256 + 16, C), bf16),
            pltpu.VMEM((UNITS, 128 + 16, C), bf16),
            pltpu.VMEM((UNITS, 128 + 16, C), bf16),
            pltpu.VMEM((UNITS, 64 + 16, C), bf16),
            pltpu.VMEM((UNITS, 64 + 16, C), bf16),
            pltpu.VMEM((UNITS, 32, C), f32),
            pltpu.VMEM((UNITS, 32, C), f32),
            pltpu.VMEM((UNITS, 128, C), f32),
            pltpu.VMEM((UNITS, 64, C), f32),
            pltpu.VMEM((UNITS, 32, C), f32),
            sem((NC,)), sem((NC,)), sem((NC,)), sem((2,)),
            sem((UNITS, NY - 1)), sem((UNITS, NY - 1)), sem((UNITS, 3)), sem((UNITS, 3)),
        ],
        compiler_params=pltpu.CompilerParams(
            collective_id=0, has_side_effects=True, vmem_limit_bytes=40 * 1024 * 1024
        ),
        cost_estimate=pl.CostEstimate(
            flops=8 * WIDTH * WIDTH * ROWS, bytes_accessed=4 * ROWS * WIDTH, transcendentals=8 * WIDTH * WIDTH
        ),
    )(frames)


def solution(mesh):
    count_tm, count_feat = mesh.shape["tm"], mesh.shape["feat"]
    out = P(("feat", "tm"), None, None)
    return jax.shard_map(
        functools.partial(shards, count_tm, count_feat),
        mesh=mesh,
        in_specs=(P("tm", "feat"),),
        out_specs=(out, out),
        check_vma=False,
    )
```

```python
import functools
import math

import jax
import jax.numpy as jnp
from jax import lax
from jax.experimental import pallas as pl
from jax.experimental.pallas import tpu as pltpu
from jax.sharding import PartitionSpec as P

LAG = 256
ROWS = 768
WIDTH = 512
NC = 4
C = WIDTH // NC
UNITS = 2 * NC
NY = 4
HALF = ROWS // 2
PEAK = 2.0**8.4
GROUPS = ((0, 1, 2, 3), (4, 5, 6), (7,))
MESH = pl.DeviceIdType.MESH


def aligned(at, n):
    return at if isinstance(at, int) else pl.multiple_of(at, n)


def encode(piece, dst, at, g, scales):
    n = piece.shape[0]
    line = lax.broadcasted_iota(jnp.int32, (16, C), 0)
    piece = piece.reshape(n // 32, 2, 16, C)
    codes = []
    for kind in range(2):
        part = piece[:, kind]
        top = jnp.max(jnp.max(jnp.abs(part), axis=0), axis=0, keepdims=True)
        scale = jnp.maximum(top, 1e-36).astype(jnp.bfloat16).astype(jnp.float32)
        scales = jnp.where(line == 2 * g + kind, scale, scales)
        unit = part * (PEAK / scale)
        third = unit * unit * unit
        sixth = third * third
        codes.append(sixth * sixth * third)
    dst[pl.ds(aligned(at, 16), n), :] = jnp.stack(codes, axis=1).reshape(n, C).astype(jnp.bfloat16)
    return scales


def decode(code, scales, g):
    n = code.shape[0]
    code = code.astype(jnp.float32)
    line = lax.broadcasted_iota(jnp.int32, (16, C), 0)
    size = jnp.exp2(jnp.log2(jnp.abs(code)) * (1.0 / 15.0))
    value = jnp.where(code > 0, size, jnp.where(code < 0, -size, 0.0)).reshape(n // 32, 2, 16, C)
    kinds = []
    for kind in range(2):
        scale = jnp.sum(jnp.where(line == 2 * g + kind, scales, 0.0), axis=0, keepdims=True)
        kinds.append(value[:, kind] * (scale * (1.0 / PEAK)))
    return jnp.stack(kinds, axis=1).reshape(n, C)


def kernel(
    norm_scale, count_tm, count_feat,
    a_hbm, inst_ref, lag_ref,
    panels, transit, left, tail, acc, ysend, yrecv, zsend1, zsend2, zsend3, zrecv1, zrecv2, zrecv3, half1, half2,
    load_sem, psend, precv, rsend, rrecv, tsem, ysem_s, ysem_r, zsem_s, zsem_r,
):
    tm, feat = lax.axis_index("tm"), lax.axis_index("feat")
    zsend, zrecv = (zsend1, zsend2, zsend3), (zrecv1, zrecv2, zrecv3)
    zl, y = tm // NY, tm % NY
    b0, b1, b2 = zl % 2, (zl // 2) % 2, zl // 4
    core, zh, x4 = feat % 2, feat // 2 % 2, feat // 4 * 4
    z = zh * 8 + zl

    def at_z(far, first, unit):
        return ((far % 8) * NY + y, first + far // 8 * 2 + unit)

    up, down = (z + 4) % 16, (z + 12) % 16
    ends = (up, down)
    starts = (down, up)
    twin = (tm, feat + 1 - 2 * core)
    relays = [at_z(far, x4, 0) for far in ends]
    sources = [at_z(far, x4, 0) for far in starts]
    onward = [
        (far % 8 * NY + y, (x4 + near // 8 * 2 + count_feat - 1) % count_feat) for far, near in zip(ends, starts)
    ]
    next_x4 = (feat + 1) % count_feat // 4 * 4
    forwarders = [at_z(far, next_x4, 0) for far in starts]
    ypeer = [((zl * NY) + (y + j) % NY, feat) for j in range(NY)]
    zpeer = [
        ((zl + step * (1 - 2 * bit)) * NY + y, feat) for step, bit in ((1, b0), (2, b1), (4, b2))
    ]

    loads = [
        pltpu.make_async_copy(a_hbm.at[:, pl.ds(c * C, C)], panels.at[c], load_sem.at[c]) for c in range(NC)
    ]
    for load in loads:
        load.start()

    barrier = pltpu.get_barrier_semaphore()
    def greet(peers):
        for peer in peers:
            pl.semaphore_signal(barrier, inc=1, device_id=peer, device_id_type=MESH)

    greet(ypeer[1:] + zpeer)

    @pl.when(core == 0)
    def _():
        greet([twin] + sources)

    @pl.when(core == 1)
    def _():
        greet(forwarders)

    @pl.when(tm > 0)
    def _():
        greet([(tm - 1, feat)])

    pl.semaphore_wait(barrier, 11 - 3 * core - (tm + 1) // count_tm)

    def half(c, way):
        return panels.at[c, pl.ds(way * HALF, HALF)]

    def pass_near(c, way):
        return pltpu.make_async_remote_copy(
            src_ref=half(c, way), dst_ref=half(NC + c, way), send_sem=psend.at[c, way], recv_sem=precv.at[c, way],
            device_id=twin, device_id_type=MESH,
        )

    def pass_far(c, way):
        return pltpu.make_async_remote_copy(
            src_ref=half(c, way), dst_ref=transit.at[c, way], send_sem=psend.at[c, way], recv_sem=rrecv.at[c, way],
            device_id=relays[way], device_id_type=MESH,
        )

    def pass_on(c, way):
        return pltpu.make_async_remote_copy(
            src_ref=transit.at[c, way], dst_ref=half(NC + c, way), send_sem=rsend.at[c, way],
            recv_sem=precv.at[c, way], device_id=onward[way], device_id_type=MESH,
        )

    def relay(c):
        @pl.when(core == 0)
        def _():
            for way in range(2):
                pass_far(c, way).wait_recv()
                pass_on(c, way).start()

    def pass_tail(target):
        return pltpu.make_async_remote_copy(
            src_ref=a_hbm.at[pl.ds(ROWS - LAG, LAG)], dst_ref=tail, send_sem=tsem.at[0], recv_sem=tsem.at[1],
            device_id=target, device_id_type=MESH,
        )

    @pl.when(tm < count_tm - 1)
    def _():
        pass_tail((tm + 1, feat)).start()

    for c in range(NC):
        loads[c].wait()

        @pl.when(core == 0)
        def _():
            for way in range(2):
                pass_far(c, way).start()

        @pl.when(core == 1)
        def _():
            for way in range(2):
                pass_near(c, way).start()

    def row_of(block, owner_y):
        bits = (block % 2) * 4 + (block // 2 % 2) * 2 + block // 4
        return owner_y * 256 + bits * 32

    def spread(cols, j, store):
        for p in range(2):
            for owner in range(NY):
                at = pl.multiple_of(row_of(2 * j + p, owner), 32)
                store(at, cols[p * 64 + owner * 16 : p * 64 + owner * 16 + 16])

    def turn(j, _):
        def store(at, piece):
            left[pl.ds(at, 16), :] = piece
            left[pl.ds(at + 16, 16), pl.ds(LAG, ROWS - LAG)] = piece[:, : ROWS - LAG]

        spread(panels[j].T, j, store)
        return 0

    lax.fori_loop(0, NC, turn, 0)

    @pl.when(tm == 0)
    def _():
        tail[...] = jnp.zeros_like(tail)

    @pl.when(tm > 0)
    def _():
        pass_tail((tm, feat)).wait_recv()

    def turn_tail(j, _):
        def store(at, piece):
            left[pl.ds(at + 16, 16), pl.ds(0, LAG)] = piece

        spread(tail[:, pl.ds(pl.multiple_of(j * C, C), C)].T, j, store)
        return 0

    lax.fori_loop(0, NC, turn_tail, 0)

    def pass_y(u, j):
        return pltpu.make_async_remote_copy(
            src_ref=ysend.at[u, j - 1], dst_ref=yrecv.at[u, j - 1], send_sem=ysem_s.at[u, j - 1],
            recv_sem=ysem_r.at[u, j - 1], device_id=(zl * NY + (y + j) % NY, feat), device_id_type=MESH,
        )

    def product(u, j):
        owner = (y + j) % NY
        rows = left[pl.ds(pl.multiple_of(owner * 256, 256), 256), :]
        return jnp.dot(rows, panels[u], preferred_element_type=jnp.float32)

    none = jnp.zeros((16, C), jnp.float32)

    def multiply(u):
        def one(j, _):
            to = ysend.at[u, j - 1]
            to[pl.ds(256, 16), :] = encode(product(u, j), to, 0, 0, none).astype(jnp.bfloat16)
            pass_y(u, j).start()
            return 0

        lax.fori_loop(1, NY, one, 0)
        acc[u] = product(u, 0)

    def sum_y(u):
        def one(j, _):
            pass_y(u, j).wait_recv()
            came = yrecv.at[u, j - 1]
            acc[u] += decode(came[pl.ds(0, 256), :], came[pl.ds(256, 16), :].astype(jnp.float32), 0)
            return 0

        lax.fori_loop(1, NY, one, 0)

    def message(buffers, k, t):
        n, ahead = 128 >> k, sum(map(len, GROUPS[:t]))
        return buffers[k].at[pl.ds(ahead * n + 16 * t, len(GROUPS[t]) * n + 16)]

    def pass_z(k, t):
        return pltpu.make_async_remote_copy(
            src_ref=message(zsend, k, t), dst_ref=message(zrecv, k, t), send_sem=zsem_s.at[k, t],
            recv_sem=zsem_r.at[k, t], device_id=zpeer[k], device_id_type=MESH,
        )

    sums = (acc, half1, half2)
    bits = (b0, b1, b2)

    def part(k, u, bit):
        n = 128 >> k
        return sums[k][u, pl.ds(pl.multiple_of(bit * n, n), n), :]

    def give(k, t):
        n, count, to = 128 >> k, len(GROUPS[t]), message(zsend, k, t)

        def one(g, scales):
            return encode(part(k, GROUPS[t][0] + g, 1 - bits[k]), to, g * n, g, scales)

        to[pl.ds(count * n, 16), :] = lax.fori_loop(0, count, one, none).astype(jnp.bfloat16)
        pass_z(k, t).start()

    def take(k, t):
        n, count, came = 128 >> k, len(GROUPS[t]), message(zrecv, k, t)
        pass_z(k, t).wait_recv()
        scales = came[pl.ds(count * n, 16), :].astype(jnp.float32)

        def total(g):
            code = came[pl.ds(aligned(g * n, 16), n), :]
            return part(k, GROUPS[t][0] + g, bits[k]) + decode(code, scales, g)

        if k < 2:

            def one(g, _):
                sums[k + 1][GROUPS[t][0] + g] = total(g)
                return 0

            lax.fori_loop(0, count, one, 0)
        else:
            for g, u in enumerate(GROUPS[t]):
                s, at = u // NC, (u % NC) * C
                done = total(g) * norm_scale
                inst_ref[:, s, pl.ds(at, C)] = done[:16]
                lag_ref[:, s, pl.ds(at, C)] = done[16:]

    def z1(t):
        give(0, t)

    def z2(t):
        take(0, t)
        give(1, t)

    def z3(t):
        take(1, t)
        give(2, t)

    def finish(t):
        take(2, t)

    def gate(_):
        @pl.when(core == 0)
        def _():
            for c in range(NC):
                for way in range(2):
                    pass_on(c, way).wait_send()

    def own_tile(c, _):
        multiply(c)
        return 0

    def next_tile(c, _):
        for way in range(2):
            pass_near(c, way).wait_recv()
        multiply(NC + c)
        return 0

    def sum_before(c, _):
        def one(u, _):
            sum_y(u)
            return 0

        lax.fori_loop(jnp.minimum(2 * c, c + 2), jnp.minimum(2 * c + 2, c + 3), one, 0)
        return 0

    lax.fori_loop(0, NC, own_tile, 0)

    @pl.when(core == 0)
    def _():
        def pass_through(c, _):
            relay(c)
            return sum_before(c, 0)

        lax.fori_loop(0, NC, next_tile, 0)
        lax.fori_loop(0, NC, pass_through, 0)

    @pl.when(core == 1)
    def _():
        def wait_for_next(c, _):
            sum_before(c, 0)
            return next_tile(c, 0)

        lax.fori_loop(0, NC, wait_for_next, 0)

    z1(0)
    sum_y(6)
    z1(1)
    sum_y(7)
    z1(2)
    for step in (z2, z3, finish):
        for t in range(len(GROUPS)):
            step(t)

    gate(0)
    for c in range(NC):
        for way in range(2):
            pass_near(c, way).wait_send()

    for u in range(UNITS):
        for j in range(1, NY):
            pass_y(u, j).wait_send()
    for k in range(3):
        for t in range(len(GROUPS)):
            pass_z(k, t).wait_send()

    @pl.when(tm < count_tm - 1)
    def _():
        pass_tail((tm + 1, feat)).wait_send()


def shards(count_tm, count_feat, frames):
    norm_scale = 1.0 / math.sqrt(ROWS * count_tm)
    f32, bf16, sem = jnp.float32, jnp.bfloat16, pltpu.SemaphoreType.DMA
    out = jax.ShapeDtypeStruct((16, 2, WIDTH), f32)
    return pl.pallas_call(
        functools.partial(kernel, norm_scale, count_tm, count_feat),
        out_shape=(out, out),
        in_specs=[pl.BlockSpec(memory_space=pl.ANY)],
        out_specs=(pl.BlockSpec(memory_space=pltpu.VMEM), pl.BlockSpec(memory_space=pltpu.VMEM)),
        scratch_shapes=[
            pltpu.VMEM((UNITS, ROWS, C), bf16),
            pltpu.VMEM((NC, 2, HALF, C), bf16),
            pltpu.VMEM((NY * 256, ROWS), bf16),
            pltpu.VMEM((LAG, WIDTH), bf16),
            pltpu.VMEM((UNITS, 256, C), f32),
            pltpu.VMEM((UNITS, NY - 1, 256 + 16, C), bf16),
            pltpu.VMEM((UNITS, NY - 1, 256 + 16, C), bf16),
            *[pltpu.VMEM((UNITS * n + 16 * len(GROUPS), C), bf16) for n in (128, 64, 32)] * 2,
            pltpu.VMEM((UNITS, 128, C), f32),
            pltpu.VMEM((UNITS, 64, C), f32),
            sem((NC,)), sem((NC, 2)), sem((NC, 2)), sem((NC, 2)), sem((NC, 2)), sem((2,)),
            sem((UNITS, NY - 1)), sem((UNITS, NY - 1)), sem((3, len(GROUPS))), sem((3, len(GROUPS))),
        ],
        compiler_params=pltpu.CompilerParams(
            collective_id=0, has_side_effects=True, vmem_limit_bytes=40 * 1024 * 1024
        ),
        cost_estimate=pl.CostEstimate(
            flops=8 * WIDTH * WIDTH * ROWS, bytes_accessed=4 * ROWS * WIDTH, transcendentals=8 * WIDTH * WIDTH
        ),
    )(frames)


def solution(mesh):
    count_tm, count_feat = mesh.shape["tm"], mesh.shape["feat"]
    out = P(("feat", "tm"), None, None)
    return jax.shard_map(
        functools.partial(shards, count_tm, count_feat),
        mesh=mesh,
        in_specs=(P("tm", "feat"),),
        out_specs=(out, out),
        check_vma=False,
    )
```

```python
import functools
import math

import jax
import jax.numpy as jnp
from jax import lax
from jax.experimental import pallas as pl
from jax.experimental.pallas import tpu as pltpu
from jax.sharding import PartitionSpec as P

LAG = 256
ROWS = 768
WIDTH = 512
NC = 4
C = WIDTH // NC
UNITS = 2 * NC
NY = 4
HALF = ROWS // 2
PEAK = 2.0**8.4
GROUPS = ((0, 1, 2, 3), (4, 5, 6), (7,))
MESH = pl.DeviceIdType.MESH


def aligned(at, n):
    return at if isinstance(at, int) else pl.multiple_of(at, n)


def encode(piece, dst, at, g, scales):
    n = piece.shape[0]
    line = lax.broadcasted_iota(jnp.int32, (16, C), 0)
    piece = piece.reshape(n // 32, 2, 16, C)
    codes = []
    for kind in range(2):
        part = piece[:, kind]
        top = jnp.max(jnp.max(jnp.abs(part), axis=0), axis=0, keepdims=True)
        scale = jnp.maximum(top, 1e-36).astype(jnp.bfloat16).astype(jnp.float32)
        scales = jnp.where(line == 2 * g + kind, scale, scales)
        unit = part * (PEAK / scale)
        third = unit * unit * unit
        sixth = third * third
        codes.append(sixth * sixth * third)
    dst[pl.ds(aligned(at, 16), n), :] = jnp.stack(codes, axis=1).reshape(n, C).astype(jnp.bfloat16)
    return scales


def decode(code, scales, g):
    n = code.shape[0]
    code = code.astype(jnp.float32)
    line = lax.broadcasted_iota(jnp.int32, (16, C), 0)
    size = jnp.exp2(jnp.log2(jnp.abs(code)) * (1.0 / 15.0))
    value = jnp.where(code > 0, size, jnp.where(code < 0, -size, 0.0)).reshape(n // 32, 2, 16, C)
    kinds = []
    for kind in range(2):
        scale = jnp.sum(jnp.where(line == 2 * g + kind, scales, 0.0), axis=0, keepdims=True)
        kinds.append(value[:, kind] * (scale * (1.0 / PEAK)))
    return jnp.stack(kinds, axis=1).reshape(n, C)


def kernel(
    norm_scale, count_tm, count_feat,
    a_hbm, inst_ref, lag_ref,
    panels, transit, left, tail, acc, ysend, yrecv, zsend1, zsend2, zsend3, zrecv1, zrecv2, zrecv3, half1, half2,
    load_sem, psend, precv, rsend, rrecv, tsem, ysem_s, ysem_r, zsem_s, zsem_r,
):
    tm, feat = lax.axis_index("tm"), lax.axis_index("feat")
    zsend, zrecv = (zsend1, zsend2, zsend3), (zrecv1, zrecv2, zrecv3)
    zl, y = tm // NY, tm % NY
    b0, b1, b2 = zl % 2, (zl // 2) % 2, zl // 4
    core, zh, x4 = feat % 2, feat // 2 % 2, feat // 4 * 4
    z = zh * 8 + zl

    def at_z(far, first, unit):
        return ((far % 8) * NY + y, first + far // 8 * 2 + unit)

    up, down = (z + 4) % 16, (z + 12) % 16
    ends = (up, down)
    starts = (down, up)
    twin = (tm, feat + 1 - 2 * core)
    relays = [at_z(far, x4, 0) for far in ends]
    sources = [at_z(far, x4, 0) for far in starts]
    onward = [
        (far % 8 * NY + y, (x4 + near // 8 * 2 + count_feat - 1) % count_feat) for far, near in zip(ends, starts)
    ]
    next_x4 = (feat + 1) % count_feat // 4 * 4
    forwarders = [at_z(far, next_x4, 0) for far in starts]
    ypeer = [((zl * NY) + (y + j) % NY, feat) for j in range(NY)]
    zpeer = [
        ((zl + step * (1 - 2 * bit)) * NY + y, feat) for step, bit in ((1, b0), (2, b1), (4, b2))
    ]

    loads = [
        pltpu.make_async_copy(a_hbm.at[:, pl.ds(c * C, C)], panels.at[c], load_sem.at[c]) for c in range(NC)
    ]
    for load in loads:
        load.start()

    barrier = pltpu.get_barrier_semaphore()
    def greet(peers):
        for peer in peers:
            pl.semaphore_signal(barrier, inc=1, device_id=peer, device_id_type=MESH)

    greet(ypeer[1:] + zpeer)

    @pl.when(core == 0)
    def _():
        greet([twin] + sources)

    @pl.when(core == 1)
    def _():
        greet(forwarders)

    @pl.when(tm > 0)
    def _():
        greet([(tm - 1, feat)])

    pl.semaphore_wait(barrier, 11 - 3 * core - (tm + 1) // count_tm)

    def half(c, way):
        return panels.at[c, pl.ds(way * HALF, HALF)]

    def pass_near(c, way):
        return pltpu.make_async_remote_copy(
            src_ref=half(c, way), dst_ref=half(NC + c, way), send_sem=psend.at[c, way], recv_sem=precv.at[c, way],
            device_id=twin, device_id_type=MESH,
        )

    def pass_far(c, way):
        return pltpu.make_async_remote_copy(
            src_ref=half(c, way), dst_ref=transit.at[c, way], send_sem=psend.at[c, way], recv_sem=rrecv.at[c, way],
            device_id=relays[way], device_id_type=MESH,
        )

    def pass_on(c, way):
        return pltpu.make_async_remote_copy(
            src_ref=transit.at[c, way], dst_ref=half(NC + c, way), send_sem=rsend.at[c, way],
            recv_sem=precv.at[c, way], device_id=onward[way], device_id_type=MESH,
        )

    def relay(c):
        @pl.when(core == 0)
        def _():
            for way in range(2):
                pass_far(c, way).wait_recv()
                pass_on(c, way).start()

    def pass_tail(target):
        return pltpu.make_async_remote_copy(
            src_ref=a_hbm.at[pl.ds(ROWS - LAG, LAG)], dst_ref=tail, send_sem=tsem.at[0], recv_sem=tsem.at[1],
            device_id=target, device_id_type=MESH,
        )

    @pl.when(tm < count_tm - 1)
    def _():
        pass_tail((tm + 1, feat)).start()

    for c in range(NC):
        loads[c].wait()

        @pl.when(core == 0)
        def _():
            for way in range(2):
                pass_far(c, way).start()

        @pl.when(core == 1)
        def _():
            for way in range(2):
                pass_near(c, way).start()

    def row_of(block, owner_y):
        bits = (block % 2) * 4 + (block // 2 % 2) * 2 + block // 4
        return owner_y * 256 + bits * 32

    def spread(cols, j, store):
        for p in range(2):
            for owner in range(NY):
                at = pl.multiple_of(row_of(2 * j + p, owner), 32)
                store(at, cols[p * 64 + owner * 16 : p * 64 + owner * 16 + 16])

    def turn(j, _):
        def store(at, piece):
            left[pl.ds(at, 16), :] = piece
            left[pl.ds(at + 16, 16), pl.ds(LAG, ROWS - LAG)] = piece[:, : ROWS - LAG]

        spread(panels[j].T, j, store)
        return 0

    lax.fori_loop(0, NC, turn, 0)

    @pl.when(tm == 0)
    def _():
        tail[...] = jnp.zeros_like(tail)

    @pl.when(tm > 0)
    def _():
        pass_tail((tm, feat)).wait_recv()

    def turn_tail(j, _):
        def store(at, piece):
            left[pl.ds(at + 16, 16), pl.ds(0, LAG)] = piece

        spread(tail[:, pl.ds(pl.multiple_of(j * C, C), C)].T, j, store)
        return 0

    lax.fori_loop(0, NC, turn_tail, 0)

    def pass_y(u, j):
        return pltpu.make_async_remote_copy(
            src_ref=ysend.at[u, j - 1], dst_ref=yrecv.at[u, j - 1], send_sem=ysem_s.at[u, j - 1],
            recv_sem=ysem_r.at[u, j - 1], device_id=(zl * NY + (y + j) % NY, feat), device_id_type=MESH,
        )

    def product(u, j):
        owner = (y + j) % NY
        rows = left[pl.ds(pl.multiple_of(owner * 256, 256), 256), :]
        return jnp.dot(rows, panels[u], preferred_element_type=jnp.float32)

    none = jnp.zeros((16, C), jnp.float32)

    def multiply(u):
        def one(j, _):
            to = ysend.at[u, j - 1]
            to[pl.ds(256, 16), :] = encode(product(u, j), to, 0, 0, none).astype(jnp.bfloat16)
            pass_y(u, j).start()
            return 0

        lax.fori_loop(1, NY, one, 0)
        acc[u] = product(u, 0)

    def sum_y(u):
        def one(j, _):
            pass_y(u, j).wait_recv()
            came = yrecv.at[u, j - 1]
            acc[u] += decode(came[pl.ds(0, 256), :], came[pl.ds(256, 16), :].astype(jnp.float32), 0)
            return 0

        lax.fori_loop(1, NY, one, 0)

    def message(buffers, k, t):
        n, ahead = 128 >> k, sum(map(len, GROUPS[:t]))
        return buffers[k].at[pl.ds(ahead * n + 16 * t, len(GROUPS[t]) * n + 16)]

    def pass_z(k, t):
        return pltpu.make_async_remote_copy(
            src_ref=message(zsend, k, t), dst_ref=message(zrecv, k, t), send_sem=zsem_s.at[k, t],
            recv_sem=zsem_r.at[k, t], device_id=zpeer[k], device_id_type=MESH,
        )

    sums = (acc, half1, half2)
    bits = (b0, b1, b2)

    def part(k, u, bit):
        n = 128 >> k
        return sums[k][u, pl.ds(pl.multiple_of(bit * n, n), n), :]

    def give(k, t):
        n, count, to = 128 >> k, len(GROUPS[t]), message(zsend, k, t)

        def one(g, scales):
            return encode(part(k, GROUPS[t][0] + g, 1 - bits[k]), to, g * n, g, scales)

        to[pl.ds(count * n, 16), :] = lax.fori_loop(0, count, one, none).astype(jnp.bfloat16)
        pass_z(k, t).start()

    def take(k, t):
        n, count, came = 128 >> k, len(GROUPS[t]), message(zrecv, k, t)
        pass_z(k, t).wait_recv()
        scales = came[pl.ds(count * n, 16), :].astype(jnp.float32)

        def total(g):
            code = came[pl.ds(aligned(g * n, 16), n), :]
            return part(k, GROUPS[t][0] + g, bits[k]) + decode(code, scales, g)

        if k < 2:

            def one(g, _):
                sums[k + 1][GROUPS[t][0] + g] = total(g)
                return 0

            lax.fori_loop(0, count, one, 0)
        else:
            for g, u in enumerate(GROUPS[t]):
                s, at = u // NC, (u % NC) * C
                done = total(g) * norm_scale
                inst_ref[:, s, pl.ds(at, C)] = done[:16]
                lag_ref[:, s, pl.ds(at, C)] = done[16:]

    def z1(t):
        give(0, t)

    def z2(t):
        take(0, t)
        give(1, t)

    def z3(t):
        take(1, t)
        give(2, t)

    def finish(t):
        take(2, t)

    def gate(_):
        @pl.when(core == 0)
        def _():
            for c in range(NC):
                for way in range(2):
                    pass_on(c, way).wait_send()

    def early0(c):
        @pl.when(c == 2)
        def _():
            z1(0)

        @pl.when(c == 3)
        def _():
            z2(0)

    def early1(c):
        @pl.when(c == 1)
        def _():
            z1(0)

        @pl.when(c == 2)
        def _():
            z2(0)

    def own_tile(c, _):
        multiply(c)
        return 0

    def next_tile(c, _):
        for way in range(2):
            pass_near(c, way).wait_recv()
        multiply(NC + c)
        return 0

    def sum_before(c, _):
        def one(u, _):
            sum_y(u)
            return 0

        lax.fori_loop(jnp.minimum(2 * c, c + 2), jnp.minimum(2 * c + 2, c + 3), one, 0)
        return 0

    lax.fori_loop(0, NC, own_tile, 0)

    @pl.when(core == 0)
    def _():
        def pass_through(c, _):
            relay(c)
            sum_before(c, 0)
            early0(c)
            return 0

        lax.fori_loop(0, NC, next_tile, 0)
        lax.fori_loop(0, NC, pass_through, 0)

    @pl.when(core == 1)
    def _():
        def wait_for_next(c, _):
            sum_before(c, 0)
            next_tile(c, 0)
            early1(c)
            return 0

        lax.fori_loop(0, NC, wait_for_next, 0)

    sum_y(6)
    z1(1)
    sum_y(7)
    z1(2)
    z2(1)
    z2(2)
    for step in (z3, finish):
        for t in range(len(GROUPS)):
            step(t)

    gate(0)
    for c in range(NC):
        for way in range(2):
            pass_near(c, way).wait_send()

    for u in range(UNITS):
        for j in range(1, NY):
            pass_y(u, j).wait_send()
    for k in range(3):
        for t in range(len(GROUPS)):
            pass_z(k, t).wait_send()

    @pl.when(tm < count_tm - 1)
    def _():
        pass_tail((tm + 1, feat)).wait_send()


def shards(count_tm, count_feat, frames):
    norm_scale = 1.0 / math.sqrt(ROWS * count_tm)
    f32, bf16, sem = jnp.float32, jnp.bfloat16, pltpu.SemaphoreType.DMA
    out = jax.ShapeDtypeStruct((16, 2, WIDTH), f32)
    return pl.pallas_call(
        functools.partial(kernel, norm_scale, count_tm, count_feat),
        out_shape=(out, out),
        in_specs=[pl.BlockSpec(memory_space=pl.ANY)],
        out_specs=(pl.BlockSpec(memory_space=pltpu.VMEM), pl.BlockSpec(memory_space=pltpu.VMEM)),
        scratch_shapes=[
            pltpu.VMEM((UNITS, ROWS, C), bf16),
            pltpu.VMEM((NC, 2, HALF, C), bf16),
            pltpu.VMEM((NY * 256, ROWS), bf16),
            pltpu.VMEM((LAG, WIDTH), bf16),
            pltpu.VMEM((UNITS, 256, C), f32),
            pltpu.VMEM((UNITS, NY - 1, 256 + 16, C), bf16),
            pltpu.VMEM((UNITS, NY - 1, 256 + 16, C), bf16),
            *[pltpu.VMEM((UNITS * n + 16 * len(GROUPS), C), bf16) for n in (128, 64, 32)] * 2,
            pltpu.VMEM((UNITS, 128, C), f32),
            pltpu.VMEM((UNITS, 64, C), f32),
            sem((NC,)), sem((NC, 2)), sem((NC, 2)), sem((NC, 2)), sem((NC, 2)), sem((2,)),
            sem((UNITS, NY - 1)), sem((UNITS, NY - 1)), sem((3, len(GROUPS))), sem((3, len(GROUPS))),
        ],
        compiler_params=pltpu.CompilerParams(
            collective_id=0, has_side_effects=True, vmem_limit_bytes=40 * 1024 * 1024
        ),
        cost_estimate=pl.CostEstimate(
            flops=8 * WIDTH * WIDTH * ROWS, bytes_accessed=4 * ROWS * WIDTH, transcendentals=8 * WIDTH * WIDTH
        ),
    )(frames)


def solution(mesh):
    count_tm, count_feat = mesh.shape["tm"], mesh.shape["feat"]
    out = P(("feat", "tm"), None, None)
    return jax.shard_map(
        functools.partial(shards, count_tm, count_feat),
        mesh=mesh,
        in_specs=(P("tm", "feat"),),
        out_specs=(out, out),
        check_vma=False,
    )
```

```python
import functools
import math

import jax
import jax.numpy as jnp
from jax import lax
from jax.experimental import pallas as pl
from jax.experimental.pallas import tpu as pltpu
from jax.sharding import PartitionSpec as P

LAG = 256
ROWS = 768
WIDTH = 512
NC = 4
C = WIDTH // NC
UNITS = 2 * NC
NY = 4
HALF = ROWS // 2
PEAK = 2.0**8.4
GROUPS = ((0, 1, 2, 3), (4, 5, 6), (7,))
MESH = pl.DeviceIdType.MESH


def aligned(at, n):
    return at if isinstance(at, int) else pl.multiple_of(at, n)


def encode(piece, dst, at, g, scales):
    n = piece.shape[0]
    line = lax.broadcasted_iota(jnp.int32, (16, C), 0)
    piece = piece.reshape(n // 32, 2, 16, C)
    codes = []
    for kind in range(2):
        part = piece[:, kind]
        top = jnp.max(jnp.max(jnp.abs(part), axis=0), axis=0, keepdims=True)
        scale = jnp.maximum(top, 1e-36).astype(jnp.bfloat16).astype(jnp.float32)
        scales = jnp.where(line == 2 * g + kind, scale, scales)
        unit = part * (PEAK / scale)
        third = unit * unit * unit
        sixth = third * third
        codes.append(sixth * sixth * third)
    dst[pl.ds(aligned(at, 16), n), :] = jnp.stack(codes, axis=1).reshape(n, C).astype(jnp.bfloat16)
    return scales


def decode(code, scales, g):
    n = code.shape[0]
    code = code.astype(jnp.float32)
    line = lax.broadcasted_iota(jnp.int32, (16, C), 0)
    size = jnp.exp2(jnp.log2(jnp.abs(code)) * (1.0 / 15.0))
    value = jnp.where(code > 0, size, jnp.where(code < 0, -size, 0.0)).reshape(n // 32, 2, 16, C)
    kinds = []
    for kind in range(2):
        scale = jnp.sum(jnp.where(line == 2 * g + kind, scales, 0.0), axis=0, keepdims=True)
        kinds.append(value[:, kind] * (scale * (1.0 / PEAK)))
    return jnp.stack(kinds, axis=1).reshape(n, C)


def kernel(
    norm_scale, count_tm, count_feat,
    a_hbm, inst_ref, lag_ref,
    panels, transit, left, tail, acc, ysend, yrecv, zsend1, zsend2, zsend3, zrecv1, zrecv2, zrecv3, half1, half2,
    load_sem, psend, precv, rsend, rrecv, tsem, ysem_s, ysem_r, zsem_s, zsem_r,
):
    tm, feat = lax.axis_index("tm"), lax.axis_index("feat")
    zsend, zrecv = (zsend1, zsend2, zsend3), (zrecv1, zrecv2, zrecv3)
    zl, y = tm // NY, tm % NY
    b0, b1, b2 = zl % 2, (zl // 2) % 2, zl // 4
    core, zh, x4 = feat % 2, feat // 2 % 2, feat // 4 * 4
    z = zh * 8 + zl

    def at_z(far, first, unit):
        return ((far % 8) * NY + y, first + far // 8 * 2 + unit)

    up, down = (z + 4) % 16, (z + 12) % 16
    ends = (up, down)
    starts = (down, up)
    twin = (tm, feat + 1 - 2 * core)
    relays = [at_z(far, x4, 0) for far in ends]
    sources = [at_z(far, x4, 0) for far in starts]
    onward = [
        (far % 8 * NY + y, (x4 + near // 8 * 2 + count_feat - 1) % count_feat) for far, near in zip(ends, starts)
    ]
    next_x4 = (feat + 1) % count_feat // 4 * 4
    forwarders = [at_z(far, next_x4, 0) for far in starts]
    ypeer = [((zl * NY) + (y + j) % NY, feat) for j in range(NY)]
    zpeer = [
        ((zl + step * (1 - 2 * bit)) * NY + y, feat) for step, bit in ((1, b0), (2, b1), (4, b2))
    ]

    loads = [
        pltpu.make_async_copy(a_hbm.at[:, pl.ds(c * C, C)], panels.at[c], load_sem.at[c]) for c in range(NC)
    ]
    for load in loads:
        load.start()

    barrier = pltpu.get_barrier_semaphore()
    def greet(peers):
        for peer in peers:
            pl.semaphore_signal(barrier, inc=1, device_id=peer, device_id_type=MESH)

    greet(ypeer[1:] + zpeer)

    @pl.when(core == 0)
    def _():
        greet([twin] + sources)

    @pl.when(core == 1)
    def _():
        greet(forwarders)

    @pl.when(tm > 0)
    def _():
        greet([(tm - 1, feat)])

    pl.semaphore_wait(barrier, 11 - 3 * core - (tm + 1) // count_tm)

    def half(c, way):
        return panels.at[c, pl.ds(way * HALF, HALF)]

    def origin(c, way):
        return a_hbm.at[pl.ds(way * HALF, HALF), pl.ds(c * C, C)]

    def pass_near(c, way):
        return pltpu.make_async_remote_copy(
            src_ref=origin(c, way), dst_ref=half(NC + c, way), send_sem=psend.at[c, way], recv_sem=precv.at[c, way],
            device_id=twin, device_id_type=MESH,
        )

    def pass_far(c, way):
        return pltpu.make_async_remote_copy(
            src_ref=origin(c, way), dst_ref=transit.at[c, way], send_sem=psend.at[c, way], recv_sem=rrecv.at[c, way],
            device_id=relays[way], device_id_type=MESH,
        )

    def pass_on(c, way):
        return pltpu.make_async_remote_copy(
            src_ref=transit.at[c, way], dst_ref=half(NC + c, way), send_sem=rsend.at[c, way],
            recv_sem=precv.at[c, way], device_id=onward[way], device_id_type=MESH,
        )

    def relay(c):
        @pl.when(core == 0)
        def _():
            for way in range(2):
                pass_far(c, way).wait_recv()
                pass_on(c, way).start()

    def pass_tail(target):
        return pltpu.make_async_remote_copy(
            src_ref=a_hbm.at[pl.ds(ROWS - LAG, LAG)], dst_ref=tail, send_sem=tsem.at[0], recv_sem=tsem.at[1],
            device_id=target, device_id_type=MESH,
        )

    @pl.when(tm < count_tm - 1)
    def _():
        pass_tail((tm + 1, feat)).start()

    for c in range(NC):

        @pl.when(core == 0)
        def _():
            for way in range(2):
                pass_far(c, way).start()

        @pl.when(core == 1)
        def _():
            for way in range(2):
                pass_near(c, way).start()

    for load in loads:
        load.wait()

    def row_of(block, owner_y):
        bits = (block % 2) * 4 + (block // 2 % 2) * 2 + block // 4
        return owner_y * 256 + bits * 32

    def spread(cols, j, store):
        for p in range(2):
            for owner in range(NY):
                at = pl.multiple_of(row_of(2 * j + p, owner), 32)
                store(at, cols[p * 64 + owner * 16 : p * 64 + owner * 16 + 16])

    def turn(j, _):
        def store(at, piece):
            left[pl.ds(at, 16), :] = piece
            left[pl.ds(at + 16, 16), pl.ds(LAG, ROWS - LAG)] = piece[:, : ROWS - LAG]

        spread(panels[j].T, j, store)
        return 0

    lax.fori_loop(0, NC, turn, 0)

    @pl.when(tm == 0)
    def _():
        tail[...] = jnp.zeros_like(tail)

    @pl.when(tm > 0)
    def _():
        pass_tail((tm, feat)).wait_recv()

    def turn_tail(j, _):
        def store(at, piece):
            left[pl.ds(at + 16, 16), pl.ds(0, LAG)] = piece

        spread(tail[:, pl.ds(pl.multiple_of(j * C, C), C)].T, j, store)
        return 0

    lax.fori_loop(0, NC, turn_tail, 0)

    def pass_y(u, j):
        return pltpu.make_async_remote_copy(
            src_ref=ysend.at[u, j - 1], dst_ref=yrecv.at[u, j - 1], send_sem=ysem_s.at[u, j - 1],
            recv_sem=ysem_r.at[u, j - 1], device_id=(zl * NY + (y + j) % NY, feat), device_id_type=MESH,
        )

    def product(u, j):
        owner = (y + j) % NY
        rows = left[pl.ds(pl.multiple_of(owner * 256, 256), 256), :]
        return jnp.dot(rows, panels[u], preferred_element_type=jnp.float32)

    none = jnp.zeros((16, C), jnp.float32)

    def multiply(u):
        def one(j, _):
            to = ysend.at[u, j - 1]
            to[pl.ds(256, 16), :] = encode(product(u, j), to, 0, 0, none).astype(jnp.bfloat16)
            pass_y(u, j).start()
            return 0

        lax.fori_loop(1, NY, one, 0)
        acc[u] = product(u, 0)

    def sum_y(u):
        def one(j, _):
            pass_y(u, j).wait_recv()
            came = yrecv.at[u, j - 1]
            acc[u] += decode(came[pl.ds(0, 256), :], came[pl.ds(256, 16), :].astype(jnp.float32), 0)
            return 0

        lax.fori_loop(1, NY, one, 0)

    def message(buffers, k, t):
        n, ahead = 128 >> k, sum(map(len, GROUPS[:t]))
        return buffers[k].at[pl.ds(ahead * n + 16 * t, len(GROUPS[t]) * n + 16)]

    def pass_z(k, t):
        return pltpu.make_async_remote_copy(
            src_ref=message(zsend, k, t), dst_ref=message(zrecv, k, t), send_sem=zsem_s.at[k, t],
            recv_sem=zsem_r.at[k, t], device_id=zpeer[k], device_id_type=MESH,
        )

    sums = (acc, half1, half2)
    bits = (b0, b1, b2)

    def part(k, u, bit):
        n = 128 >> k
        return sums[k][u, pl.ds(pl.multiple_of(bit * n, n), n), :]

    def give(k, t):
        n, count, to = 128 >> k, len(GROUPS[t]), message(zsend, k, t)

        def one(g, scales):
            return encode(part(k, GROUPS[t][0] + g, 1 - bits[k]), to, g * n, g, scales)

        to[pl.ds(count * n, 16), :] = lax.fori_loop(0, count, one, none).astype(jnp.bfloat16)
        pass_z(k, t).start()

    def take(k, t):
        n, count, came = 128 >> k, len(GROUPS[t]), message(zrecv, k, t)
        pass_z(k, t).wait_recv()
        scales = came[pl.ds(count * n, 16), :].astype(jnp.float32)

        def total(g):
            code = came[pl.ds(aligned(g * n, 16), n), :]
            return part(k, GROUPS[t][0] + g, bits[k]) + decode(code, scales, g)

        if k < 2:

            def one(g, _):
                sums[k + 1][GROUPS[t][0] + g] = total(g)
                return 0

            lax.fori_loop(0, count, one, 0)
        else:
            for g, u in enumerate(GROUPS[t]):
                s, at = u // NC, (u % NC) * C
                done = total(g) * norm_scale
                inst_ref[:, s, pl.ds(at, C)] = done[:16]
                lag_ref[:, s, pl.ds(at, C)] = done[16:]

    def z1(t):
        give(0, t)

    def z2(t):
        take(0, t)
        give(1, t)

    def z3(t):
        take(1, t)
        give(2, t)

    def finish(t):
        take(2, t)

    def gate(_):
        @pl.when(core == 0)
        def _():
            for c in range(NC):
                for way in range(2):
                    pass_on(c, way).wait_send()

    def early0(c):
        @pl.when(c == 2)
        def _():
            z1(0)

        @pl.when(c == 3)
        def _():
            z2(0)

    def early1(c):
        @pl.when(c == 1)
        def _():
            z1(0)

        @pl.when(c == 2)
        def _():
            z2(0)

    def own_tile(c, _):
        multiply(c)
        return 0

    def next_tile(c, _):
        for way in range(2):
            pass_near(c, way).wait_recv()
        multiply(NC + c)
        return 0

    def sum_before(c, _):
        def one(u, _):
            sum_y(u)
            return 0

        lax.fori_loop(jnp.minimum(2 * c, c + 2), jnp.minimum(2 * c + 2, c + 3), one, 0)
        return 0

    lax.fori_loop(0, NC, own_tile, 0)

    @pl.when(core == 0)
    def _():
        def pass_through(c, _):
            relay(c)
            sum_before(c, 0)
            early0(c)
            return 0

        lax.fori_loop(0, NC, next_tile, 0)
        lax.fori_loop(0, NC, pass_through, 0)

    @pl.when(core == 1)
    def _():
        def wait_for_next(c, _):
            sum_before(c, 0)
            next_tile(c, 0)
            early1(c)
            return 0

        lax.fori_loop(0, NC, wait_for_next, 0)

    sum_y(6)
    z1(1)
    sum_y(7)
    z1(2)
    z2(1)
    z2(2)
    for step in (z3, finish):
        for t in range(len(GROUPS)):
            step(t)

    gate(0)
    for c in range(NC):
        for way in range(2):
            pass_near(c, way).wait_send()

    for u in range(UNITS):
        for j in range(1, NY):
            pass_y(u, j).wait_send()
    for k in range(3):
        for t in range(len(GROUPS)):
            pass_z(k, t).wait_send()

    @pl.when(tm < count_tm - 1)
    def _():
        pass_tail((tm + 1, feat)).wait_send()


def shards(count_tm, count_feat, frames):
    norm_scale = 1.0 / math.sqrt(ROWS * count_tm)
    f32, bf16, sem = jnp.float32, jnp.bfloat16, pltpu.SemaphoreType.DMA
    out = jax.ShapeDtypeStruct((16, 2, WIDTH), f32)
    return pl.pallas_call(
        functools.partial(kernel, norm_scale, count_tm, count_feat),
        out_shape=(out, out),
        in_specs=[pl.BlockSpec(memory_space=pl.ANY)],
        out_specs=(pl.BlockSpec(memory_space=pltpu.VMEM), pl.BlockSpec(memory_space=pltpu.VMEM)),
        scratch_shapes=[
            pltpu.VMEM((UNITS, ROWS, C), bf16),
            pltpu.VMEM((NC, 2, HALF, C), bf16),
            pltpu.VMEM((NY * 256, ROWS), bf16),
            pltpu.VMEM((LAG, WIDTH), bf16),
            pltpu.VMEM((UNITS, 256, C), f32),
            pltpu.VMEM((UNITS, NY - 1, 256 + 16, C), bf16),
            pltpu.VMEM((UNITS, NY - 1, 256 + 16, C), bf16),
            *[pltpu.VMEM((UNITS * n + 16 * len(GROUPS), C), bf16) for n in (128, 64, 32)] * 2,
            pltpu.VMEM((UNITS, 128, C), f32),
            pltpu.VMEM((UNITS, 64, C), f32),
            sem((NC,)), sem((NC, 2)), sem((NC, 2)), sem((NC, 2)), sem((NC, 2)), sem((2,)),
            sem((UNITS, NY - 1)), sem((UNITS, NY - 1)), sem((3, len(GROUPS))), sem((3, len(GROUPS))),
        ],
        compiler_params=pltpu.CompilerParams(
            collective_id=0, has_side_effects=True, vmem_limit_bytes=40 * 1024 * 1024
        ),
        cost_estimate=pl.CostEstimate(
            flops=8 * WIDTH * WIDTH * ROWS, bytes_accessed=4 * ROWS * WIDTH, transcendentals=8 * WIDTH * WIDTH
        ),
    )(frames)


def solution(mesh):
    count_tm, count_feat = mesh.shape["tm"], mesh.shape["feat"]
    out = P(("feat", "tm"), None, None)
    return jax.shard_map(
        functools.partial(shards, count_tm, count_feat),
        mesh=mesh,
        in_specs=(P("tm", "feat"),),
        out_specs=(out, out),
        check_vma=False,
    )
```
